32 devices in a mesh: groups: 1, ffn: 32 (over z, y, x, core), mp: 1.
Axes of the slice: x: 2, y: 2, z: 4, core: 2. Of those that a mesh axis runs over, the one named last changes fastest.
Arguments:
- hidden_in: bfloat16 [128, 4096], P(('groups', 'ffn'), 'mp'), may hold values from -6 to 6
- out_grad: bfloat16 [128, 4096], P(('groups', 'ffn'), 'mp'), may hold values from -0.796875 to 0.796875
- step_ids: int32 [128], P(('groups', 'ffn')), may hold values from 0 to 7
- segment_ids: int32 [128], P(('groups', 'ffn')), may hold values from 0 to 3, never falling along the last dimension, each value on 1 to 64 neighbouring positions
- advantage_codes: int32 [128], P(('groups', 'ffn')), may hold values from -8 to 8
- gate_weight: bfloat16 [4096, 7168], P('mp', 'ffn'), may hold values from -0.09375 to 0.09375
- up_weight: bfloat16 [4096, 7168], P('mp', 'ffn'), may hold values from -0.09375 to 0.09375
- down_weight: bfloat16 [7168, 4096], P('ffn', 'mp'), may hold values from -0.0625 to 0.0625
Outputs:
- input_grad: bfloat16 [128, 4096], P(('groups', 'ffn'), 'mp')
- gate_grad: bfloat16 [4096, 7168], P(('groups', 'mp'), 'ffn')
- up_grad: bfloat16 [4096, 7168], P(('groups', 'mp'), 'ffn')
- down_grad: bfloat16 [7168, 4096], P(('groups', 'ffn'), 'mp')
The draws below stay inside these ranges and needn't reach their ends.
All inputs are finite; a program needn't handle non-finite values.
Results may differ from the reference program's by a relative error of at most 0.0057.
Values may be sent and summed in bfloat16 or wider, within the bound.
A program may use at most 64 MiB of HBM per device.

```python
import math
import jax
import jax.numpy as jnp
import numpy as np
from jax import lax

D = 4096
FF = 7168
TOKENS = 128


def plant(array, own_key, smallest, top_value):
    longest = array.shape.index(max(array.shape))
    spots = []
    for shift in (0, 1):
        where = [jax.random.randint(jax.random.fold_in(own_key, axis), (), 0, length) for axis, length in enumerate(array.shape)]
        where[longest] = (where[longest] + shift) % array.shape[longest]
        spots.append(tuple(where))
    return array.at[spots[0]].set(smallest).at[spots[1]].set(top_value)


def levels(rng, extent, split, low, high):
    def one(dim, shards_of):
        steps = jax.random.uniform(jax.random.fold_in(jax.random.fold_in(rng, 6), dim), (shards_of,), jnp.float32, low / len(split), high / len(split))
        return jnp.repeat(jnp.exp(steps), extent[dim] // shards_of).reshape((-1,) + (1,) * (len(extent) - dim - 1))

    factor_of = one(*split[0])
    for cut in split[1:]:
        factor_of = factor_of * one(*cut)
    return factor_of


def profile(amount, total, reach, skew):
    portions = [(1 << 20) // math.isqrt(grade ** skew) + 1 for grade in range(2, amount + 1)]
    rest, counts = total - reach - (amount - 1), [1] * (amount - 1)
    while rest > 0:
        candidates = [i for i in range(amount - 1) if counts[i] < reach]
        pool, remaining = sum([portions[i] for i in candidates]), rest
        for i in candidates:
            extra = min(reach - counts[i], max(1, remaining * portions[i] // pool), rest)
            counts[i] = counts[i] + extra
            rest = rest - extra
    return np.array([reach] + counts)


def ragged_sizes(own_key, number_of, total, reach, lean):
    if number_of == 2:
        one = jax.random.randint(own_key, (), max(1, total - reach), min(reach, total - 1) + 1)
        return jnp.stack([one, total - one])
    sizes = jnp.asarray(profile(number_of, total, reach, lean), jnp.int32)
    pairs = (number_of - 1) // 2
    giver, taker = sizes[1:1 + 2 * pairs:2], sizes[2:2 + 2 * pairs:2]
    room = jnp.minimum(giver - 1, reach - taker)
    moved = jax.random.randint(jax.random.fold_in(own_key, 1), (pairs,), 0, 1 << 20) % (room + 1)
    sizes = sizes.at[1:1 + 2 * pairs:2].set(giver - moved).at[2:2 + 2 * pairs:2].set(taker + moved)
    return sizes[jax.random.permutation(jax.random.fold_in(own_key, 2), number_of)]


def scatter_about(key, extent, deviation, limit, split=(), kind=jnp.bfloat16):
    level = levels(key, extent, split, -0.22, 0.18) if split else 1.0
    drawn = jax.random.normal(key, extent, jnp.float32) * deviation * level
    return jnp.minimum(jnp.maximum(drawn, -limit), limit).astype(kind)


def setup_inputs(seed: int = 0, part: int = 0) -> dict:
    seeds = jax.random.split(jax.random.key(seed), 9)
    part_splits = jax.random.split(jax.random.fold_in(seeds[8], part), 9)
    return {
        "hidden_in": scatter_about(part_splits[0], (TOKENS, D), 1.0, 6.0, ((0, 32),)),
        "out_grad": scatter_about(part_splits[1], (TOKENS, D), 0.1, 0.796875, ((0, 32),)),
        "step_ids": plant(jax.random.randint(part_splits[2], (TOKENS,), 0, 8), jax.random.fold_in(part_splits[2], 1), 0, 7).astype(jnp.int32),
        "segment_ids": jnp.searchsorted(jnp.cumsum(ragged_sizes(part_splits[3], TOKENS // 32, TOKENS, 64, 1)), jnp.arange(TOKENS), side="right").astype(jnp.int32),
        "advantage_codes": plant(jax.random.randint(part_splits[4], (TOKENS,), -8, 9), jax.random.fold_in(part_splits[4], 1), -8, 8).astype(jnp.int32),
        "gate_weight": scatter_about(seeds[5], (D, FF), D ** -0.5, 0.09375, ((1, 32),)),
        "up_weight": scatter_about(seeds[6], (D, FF), D ** -0.5, 0.09375, ((1, 32),)),
        "down_weight": scatter_about(seeds[7], (FF, D), FF ** -0.5, 0.0625, ((0, 32),)),
    }


def advantage_weights(steps, segments, codes):
    same = segments[:, None] == segments[None, :]
    later = steps[None, :] >= steps[:, None]
    gap = (steps[None, :] - steps[:, None]).astype(jnp.float32)
    kernel = jnp.where(same & later, jnp.exp(gap * math.log(0.75)), jnp.zeros_like(gap))
    total = jnp.dot(kernel, codes.astype(jnp.float32), precision=lax.Precision.HIGHEST)
    count = lax.optimization_barrier(jnp.sum(same.astype(jnp.float32), axis=1))
    return total / (8.0 * jnp.sqrt(count))

def reference(hidden_in, out_grad, step_ids, segment_ids, advantage_codes, gate_weight, up_weight, down_weight):
    advantage = advantage_weights(step_ids, segment_ids, advantage_codes)
    weighted = (advantage[:, None] * out_grad.astype(jnp.float32)).astype(jnp.bfloat16)
    gate_pre = jnp.dot(hidden_in, gate_weight, preferred_element_type=jnp.float32)
    up_pre = jnp.dot(hidden_in, up_weight, preferred_element_type=jnp.float32)
    sigma = jax.nn.sigmoid(gate_pre)
    hidden = (gate_pre * sigma * up_pre).astype(jnp.bfloat16)
    hidden_grad = jnp.dot(weighted, down_weight.T, preferred_element_type=jnp.float32)
    up_delta = (hidden_grad * gate_pre * sigma).astype(jnp.bfloat16)
    gate_delta = (hidden_grad * up_pre * sigma * (1.0 + gate_pre * (1.0 - sigma))).astype(jnp.bfloat16)
    down_grad = jnp.dot(hidden.T, weighted, preferred_element_type=jnp.float32).astype(jnp.bfloat16)
    gate_grad = jnp.dot(hidden_in.T, gate_delta, preferred_element_type=jnp.float32).astype(jnp.bfloat16)
    up_grad = jnp.dot(hidden_in.T, up_delta, preferred_element_type=jnp.float32).astype(jnp.bfloat16)
    input_grad = jnp.dot(gate_delta, gate_weight.T, preferred_element_type=jnp.float32)
    input_grad = input_grad + jnp.dot(up_delta, up_weight.T, preferred_element_type=jnp.float32)
    return (input_grad.astype(jnp.bfloat16), gate_grad, up_grad, down_grad)
```

```python
import math

import jax
import jax.numpy as jnp
from jax import lax
from jax.experimental import pallas as pl
from jax.experimental.pallas import tpu as pltpu
from jax.sharding import PartitionSpec as P


def advantage_weights(steps, segments, codes):
    same = segments[:, None] == segments[None, :]
    later = steps[None, :] >= steps[:, None]
    gap = (steps[None, :] - steps[:, None]).astype(jnp.float32)
    kernel = jnp.where(same & later, jnp.exp(gap * math.log(0.75)), jnp.zeros_like(gap))
    total = jnp.dot(kernel, codes.astype(jnp.float32), precision=lax.Precision.HIGHEST)
    count = jnp.sum(same.astype(jnp.float32), axis=1)
    return total / (8.0 * jnp.sqrt(count))


def contract_last(left, right):
    return lax.dot_general(
        left, right, (((1,), (1,)), ((), ())), preferred_element_type=jnp.float32
    )


def contract_first(left, right):
    return lax.dot_general(
        left, right, (((0,), (0,)), ((), ())), preferred_element_type=jnp.float32
    )


BF = jnp.bfloat16
F32 = jnp.float32
MESH = pl.DeviceIdType.MESH
LANES = 128


def gather_kernel(
    x_ref, g_ref, step_ref, segment_ref, code_ref, gate_hbm, up_hbm, down_hbm,
    input_grad_ref, x_out, weighted_out, hidden_out, gate_delta_out, up_delta_out,
    gate_w, up_w, down_w, raw, rows, part, core_out, core_in, sums, first_out, first_in,
    halves, second_out, second_in, blocks, last_keep, last_out, last_in,
    weight_sem, up_send, up_recv, dn_send, dn_recv, l_send, l_recv,
    core_send, core_recv, first_send, first_recv, second_send, second_recv, z_send, z_recv,
):
    features = x_ref.shape[1]
    wide = features // 4
    me = lax.axis_index("ffn")
    z = me // 8
    y = lax.rem(me // 4, 2)
    x = lax.rem(me // 2, 2)
    core = lax.rem(me, 2)
    mate = me + 1 - 2 * core
    xnbr = me + 2 - 4 * x
    ynbr = me + 4 - 8 * y

    loads = [
        pltpu.make_async_copy(src, dst, weight_sem.at[i])
        for i, (src, dst) in enumerate(((gate_hbm, gate_w), (up_hbm, up_w), (down_hbm, down_w)))
    ]
    for load in loads:
        load.start()

    def remote(src, dst, send, recv, target):
        return pltpu.make_async_remote_copy(
            src_ref=src, dst_ref=dst, send_sem=send, recv_sem=recv,
            device_id={"ffn": target}, device_id_type=MESH,
        )

    barrier = pltpu.get_barrier_semaphore()
    zpeers = [lax.rem(z + d, 4) * 8 + lax.rem(me, 8) for d in (1, 2, 3)]
    for partner in [mate, xnbr, ynbr] + zpeers:
        pl.semaphore_signal(barrier, inc=1, device_id={"ffn": partner}, device_id_type=MESH)

    row = lax.broadcasted_iota(jnp.int32, (16, LANES), 0)
    lane = lax.broadcasted_iota(jnp.int32, (16, LANES), 1)
    labels = jnp.zeros((16, LANES), F32)
    for t in range(4):
        for k, ref in enumerate((step_ref, segment_ref, code_ref)):
            labels = jnp.where((row == t) & (lane == k), ref[t].astype(F32), labels)

    def fold(ref):
        full = ref[...].astype(F32)
        return jnp.concatenate([full[:, c * wide:(c + 1) * wide] for c in range(4)], axis=0)

    raw[z, :, 0:LANES] = labels.astype(BF)
    raw[z, :, LANES:LANES + wide] = fold(x_ref).astype(BF)
    raw[z, :, LANES + wide:LANES + 2 * wide] = fold(g_ref).astype(BF)
    pl.semaphore_wait(barrier, 6)

    def upward(s, block):
        return remote(raw.at[block], raw.at[block], up_send.at[s], up_recv.at[s], me + 8)

    def downward(s, block):
        return remote(raw.at[block], raw.at[block], dn_send.at[s], dn_recv.at[s], me - 8)

    for s in range(3):
        @pl.when((z < 3) & (z - s >= 0))
        def _(s=s):
            upward(s, z - s).start()

        @pl.when((z > 0) & (z + s <= 3))
        def _(s=s):
            downward(s, z + s).start()

        @pl.when(z - 1 - s >= 0)
        def _(s=s):
            upward(s, z - 1 - s).wait_recv()

        @pl.when(z + 1 + s <= 3)
        def _(s=s):
            downward(s, z + 1 + s).wait_recv()

    mine = core * 4 + x * 2 + y
    by_y = core * 4 + x * 2 + 1 - y
    by_x = core * 4 + (1 - x) * 2 + y
    diag = core * 4 + (1 - x) * 2 + 1 - y
    flip = 4 - 8 * core
    xp = pl.ds(0, LANES + features)
    gp = pl.ds(LANES + features, features)

    pieces = [raw[k].astype(F32) for k in range(4)]
    rows[mine, :, 0:LANES] = jnp.concatenate(
        [piece[0:4, 0:LANES] for piece in pieces], axis=0
    ).astype(BF)
    for a in range(2):
        for c in range(4):
            lo = LANES + a * wide
            out = LANES + a * features + c * wide
            rows[mine, :, out:out + wide] = jnp.concatenate(
                [piece[4 * c:4 * c + 4, lo:lo + wide] for piece in pieces], axis=0
            ).astype(BF)

    def plane(i, block, columns, target):
        view = rows.at[block] if columns is None else rows.at[block, :, columns]
        return remote(view, view, l_send.at[i], l_recv.at[i], target)

    sends = [
        plane(0, mine, xp, ynbr),
        plane(1, mine, gp, xnbr),
        plane(2, mine, xp, xnbr),
        plane(3, mine, gp, ynbr),
        plane(4, mine, None, mate),
        plane(5, by_y, xp, xnbr),
        plane(6, by_x, gp, ynbr),
        plane(7, by_x, None, mate),
        plane(8, by_y, None, mate),
        plane(9, diag, None, mate),
    ]
    takes = [
        plane(0, by_y, xp, ynbr),
        plane(1, by_x, gp, xnbr),
        plane(2, by_x, xp, xnbr),
        plane(3, by_y, gp, ynbr),
        plane(4, mine + flip, None, mate),
        plane(5, diag, xp, xnbr),
        plane(6, diag, gp, ynbr),
        plane(7, by_x + flip, None, mate),
        plane(8, by_y + flip, None, mate),
        plane(9, diag + flip, None, mate),
    ]
    for i in range(5):
        sends[i].start()
    takes[0].wait_recv()
    sends[5].start()
    takes[1].wait_recv()
    sends[6].start()
    takes[2].wait_recv()
    sends[7].start()
    takes[3].wait_recv()
    sends[8].start()
    takes[5].wait_recv()
    takes[6].wait_recv()
    sends[9].start()
    for i in (4, 7, 8, 9):
        takes[i].wait_recv()

    tokens = 8 * 16
    tags = rows[:, :, 0:LANES].reshape(tokens, LANES)
    pick = (
        lax.broadcasted_iota(jnp.int32, (16, LANES), 0)
        == lax.broadcasted_iota(jnp.int32, (16, LANES), 1)
    ).astype(F32).astype(BF)
    across = contract_last(pick, tags)
    down = tags.astype(F32)
    gap = across[0:1, :] - down[:, 0:1]
    same = across[1:2, :] == down[:, 1:2]
    decay = jnp.where(same & (gap >= 0.0), jnp.exp(gap * math.log(0.75)), 0.0)
    total = jnp.sum(decay * across[2:3, :], axis=1, keepdims=True)
    count = jnp.sum(jnp.where(same, 1.0, 0.0), axis=1, keepdims=True)
    advantage = total / (8.0 * jnp.sqrt(count))

    for load in loads:
        load.wait()
    gate_pre = jnp.zeros((tokens, gate_w.shape[1]), F32)
    up_pre = jnp.zeros((tokens, gate_w.shape[1]), F32)
    hidden_grad = jnp.zeros((tokens, gate_w.shape[1]), F32)
    for c in range(4):
        cols = slice(c * wide, (c + 1) * wide)
        xs = rows[:, :, LANES + c * wide:LANES + (c + 1) * wide].reshape(tokens, wide)
        x_out[:, cols] = xs
        gate_pre += jnp.dot(xs, gate_w[cols, :], preferred_element_type=F32)
        up_pre += jnp.dot(xs, up_w[cols, :], preferred_element_type=F32)
        lo = LANES + features + c * wide
        gs = rows[:, :, lo:lo + wide].reshape(tokens, wide)
        weighted = (advantage * gs.astype(F32)).astype(BF)
        weighted_out[:, cols] = weighted
        hidden_grad += contract_last(weighted, down_w[:, cols])
    sigma = 1.0 / (1.0 + jnp.exp(-gate_pre))
    hidden_out[...] = (gate_pre * sigma * up_pre).astype(BF)
    up_delta = (hidden_grad * gate_pre * sigma).astype(BF)
    gate_delta = (hidden_grad * up_pre * sigma * (1.0 + gate_pre * (1.0 - sigma))).astype(BF)
    up_delta_out[...] = up_delta
    gate_delta_out[...] = gate_delta

    for k in range(4):
        cols = slice(k * wide, (k + 1) * wide)
        share = contract_last(gate_delta, gate_w[cols, :]) + contract_last(up_delta, up_w[cols, :])
        part[k] = share.reshape(8, 16, wide)
        core_out[k] = part[k, pl.ds((1 - core) * 4, 4)].astype(BF)
        remote(core_out.at[k], core_in.at[k], core_send.at[k], core_recv.at[k], mate).start()

    def first(k):
        return remote(
            first_out.at[k], first_in.at[k], first_send.at[k], first_recv.at[k],
            xnbr if k % 2 == 0 else ynbr,
        )

    def second(k):
        return remote(
            second_out.at[k], second_in.at[k], second_send.at[k], second_recv.at[k],
            ynbr if k % 2 == 0 else xnbr,
        )

    for k in range(4):
        remote(core_out.at[k], core_in.at[k], core_send.at[k], core_recv.at[k], mate).wait_recv()
        sums[k] = part[k, pl.ds(core * 4, 4)] + core_in[k].astype(F32)
        for j in range(2):
            other = (1 - x) * 2 + j if k % 2 == 0 else j * 2 + 1 - y
            first_out[k, j] = sums[k, other].astype(BF)
        first(k).start()
    for k in range(4):
        first(k).wait_recv()
        for j in range(2):
            own = x * 2 + j if k % 2 == 0 else j * 2 + y
            halves[k, j] = sums[k, own] + first_in[k, j].astype(F32)
        side = y if k % 2 == 0 else x
        second_out[k] = halves[k, 1 - side].astype(BF)
        second(k).start()
    for k in range(4):
        second(k).wait_recv()
        side = y if k % 2 == 0 else x
        blocks[k] = halves[k, side] + second_in[k].astype(F32)
    stripes = [blocks[k] for k in range(4)]
    for zz in range(4):
        folded = jnp.concatenate([stripe[4 * zz:4 * zz + 4, :] for stripe in stripes], axis=0)
        last_keep[zz] = folded
        last_out[zz] = folded.astype(BF)

    def last(d):
        there = lax.rem(z + d, 4)
        return remote(
            last_out.at[there], last_in.at[d - 1], z_send.at[d - 1], z_recv.at[d - 1],
            there * 8 + lax.rem(me, 8),
        )

    for d in (1, 2, 3):
        last(d).start()
    for d in (1, 2, 3):
        last(d).wait_recv()
    final = last_keep[z] + last_in[0].astype(F32) + last_in[1].astype(F32) + last_in[2].astype(F32)
    for k in range(4):
        input_grad_ref[:, k * wide:(k + 1) * wide] = final[4 * k:4 * k + 4, :].astype(BF)

    for s in range(3):
        @pl.when((z < 3) & (z - s >= 0))
        def _(s=s):
            upward(s, z - s).wait_send()

        @pl.when((z > 0) & (z + s <= 3))
        def _(s=s):
            downward(s, z + s).wait_send()
    for send in sends:
        send.wait_send()
    for k in range(4):
        remote(core_out.at[k], core_in.at[k], core_send.at[k], core_recv.at[k], mate).wait_send()
        first(k).wait_send()
        second(k).wait_send()
    for d in (1, 2, 3):
        last(d).wait_send()


def fused(
    hidden_in, out_grad, step_ids, segment_ids, advantage_codes, gate_weight, up_weight, down_weight
):
    features, units = gate_weight.shape
    tokens = 32 * hidden_in.shape[0]
    wide = features // 4
    vmem = pl.BlockSpec(memory_space=pltpu.VMEM)
    smem = pl.BlockSpec(memory_space=pltpu.SMEM)
    hbm = pl.BlockSpec(memory_space=pl.ANY)
    dma = pltpu.SemaphoreType.DMA
    input_grad, inputs_all, weighted, hidden, gate_delta, up_delta = pl.pallas_call(
        gather_kernel,
        out_shape=(
            jax.ShapeDtypeStruct(hidden_in.shape, BF),
            jax.ShapeDtypeStruct((tokens, features), BF),
            jax.ShapeDtypeStruct((tokens, features), BF),
            jax.ShapeDtypeStruct((tokens, units), BF),
            jax.ShapeDtypeStruct((tokens, units), BF),
            jax.ShapeDtypeStruct((tokens, units), BF),
        ),
        in_specs=[vmem, vmem, smem, smem, smem, hbm, hbm, hbm],
        out_specs=(vmem,) * 6,
        scratch_shapes=[
            pltpu.VMEM((features, units), BF),
            pltpu.VMEM((features, units), BF),
            pltpu.VMEM((units, features), BF),
            pltpu.VMEM((4, 16, LANES + 2 * wide), BF),
            pltpu.VMEM((8, 16, LANES + 2 * features), BF),
            pltpu.VMEM((4, 8, 16, wide), F32),
            pltpu.VMEM((4, 4, 16, wide), BF),
            pltpu.VMEM((4, 4, 16, wide), BF),
            pltpu.VMEM((4, 4, 16, wide), F32),
            pltpu.VMEM((4, 2, 16, wide), BF),
            pltpu.VMEM((4, 2, 16, wide), BF),
            pltpu.VMEM((4, 2, 16, wide), F32),
            pltpu.VMEM((4, 16, wide), BF),
            pltpu.VMEM((4, 16, wide), BF),
            pltpu.VMEM((4, 16, wide), F32),
            pltpu.VMEM((4, 16, wide), F32),
            pltpu.VMEM((4, 16, wide), BF),
            pltpu.VMEM((3, 16, wide), BF),
            dma((3,)),
            dma((3,)), dma((3,)), dma((3,)), dma((3,)),
            dma((10,)), dma((10,)),
            dma((4,)), dma((4,)), dma((4,)), dma((4,)), dma((4,)), dma((4,)),
            dma((3,)), dma((3,)),
        ],
        compiler_params=pltpu.CompilerParams(
            collective_id=0, has_side_effects=True, vmem_limit_bytes=48 * 1024 * 1024
        ),
        cost_estimate=pl.CostEstimate(
            flops=10 * tokens * features * units, bytes_accessed=6 * features * units, transcendentals=0
        ),
        name="gather_and_sum",
    )(
        hidden_in, out_grad, step_ids, segment_ids, advantage_codes,
        gate_weight, up_weight, down_weight,
    )
    down_grad = contract_first(hidden, weighted).astype(BF)
    gate_grad = contract_first(inputs_all, gate_delta).astype(BF)
    up_grad = contract_first(inputs_all, up_delta).astype(BF)
    return (input_grad, gate_grad, up_grad, down_grad)


def local(
    hidden_in, out_grad, step_ids, segment_ids, advantage_codes, gate_weight, up_weight, down_weight
):
    inputs_all, grads_all = (
        lax.all_gather(hidden_in, "ffn", axis=0, tiled=True),
        lax.all_gather(out_grad, "ffn", axis=0, tiled=True),
    )
    labels = lax.all_gather(
        jnp.stack([step_ids, segment_ids, advantage_codes]), "ffn", axis=1, tiled=True
    )
    advantage = advantage_weights(labels[0], labels[1], labels[2])
    weighted = (advantage[:, None] * grads_all.astype(jnp.float32)).astype(jnp.bfloat16)
    gate_part = jnp.dot(inputs_all, gate_weight, preferred_element_type=jnp.float32)
    up_part = jnp.dot(inputs_all, up_weight, preferred_element_type=jnp.float32)
    gate_pre, up_pre = lax.psum((gate_part, up_part), "mp")
    sigma = jax.nn.sigmoid(gate_pre)
    hidden = (gate_pre * sigma * up_pre).astype(jnp.bfloat16)
    hidden_grad = lax.psum(contract_last(weighted, down_weight), "mp")
    up_delta = (hidden_grad * gate_pre * sigma).astype(jnp.bfloat16)
    gate_delta = (hidden_grad * up_pre * sigma * (1.0 + gate_pre * (1.0 - sigma))).astype(
        jnp.bfloat16
    )
    down_grad = contract_first(hidden, weighted).astype(jnp.bfloat16)
    gate_grad = contract_first(inputs_all, gate_delta).astype(jnp.bfloat16)
    up_grad = contract_first(inputs_all, up_delta).astype(jnp.bfloat16)
    partial_grad = contract_last(gate_delta, gate_weight) + contract_last(up_delta, up_weight)
    input_grad = lax.psum_scatter(partial_grad, "ffn", scatter_dimension=0, tiled=True)
    return (input_grad.astype(jnp.bfloat16), gate_grad, up_grad, down_grad)


def solution(mesh):
    in_specs = (
        P(("groups", "ffn"), "mp"),
        P(("groups", "ffn"), "mp"),
        P(("groups", "ffn")),
        P(("groups", "ffn")),
        P(("groups", "ffn")),
        P("mp", "ffn"),
        P("mp", "ffn"),
        P("ffn", "mp"),
    )
    out_specs = (
        P(("groups", "ffn"), "mp"),
        P(("groups", "mp"), "ffn"),
        P(("groups", "mp"), "ffn"),
        P(("groups", "ffn"), "mp"),
    )
    whole = mesh.shape["groups"] == 1 and mesh.shape["mp"] == 1 and mesh.shape["ffn"] == 32
    return jax.shard_map(fused if whole else local, mesh=mesh, in_specs=in_specs, out_specs=out_specs, check_vma=False)
```

```python
import math

import jax
import jax.numpy as jnp
from jax import lax
from jax.experimental import pallas as pl
from jax.experimental.pallas import tpu as pltpu
from jax.sharding import PartitionSpec as P


def advantage_weights(steps, segments, codes):
    same = segments[:, None] == segments[None, :]
    later = steps[None, :] >= steps[:, None]
    gap = (steps[None, :] - steps[:, None]).astype(jnp.float32)
    kernel = jnp.where(same & later, jnp.exp(gap * math.log(0.75)), jnp.zeros_like(gap))
    total = jnp.dot(kernel, codes.astype(jnp.float32), precision=lax.Precision.HIGHEST)
    count = jnp.sum(same.astype(jnp.float32), axis=1)
    return total / (8.0 * jnp.sqrt(count))


def contract_last(left, right):
    return lax.dot_general(
        left, right, (((1,), (1,)), ((), ())), preferred_element_type=jnp.float32
    )


def contract_first(left, right):
    return lax.dot_general(
        left, right, (((0,), (0,)), ((), ())), preferred_element_type=jnp.float32
    )


BF = jnp.bfloat16
F32 = jnp.float32
MESH = pl.DeviceIdType.MESH
LANES = 128


def gather_kernel(
    x_ref, g_ref, step_ref, segment_ref, code_ref, gate_hbm, up_hbm, down_hbm,
    input_grad_ref, gate_grad_ref, up_grad_ref, down_grad_ref,
    gate_w, up_w, down_w, weighted_all, raw, rows, part, core_out, core_in, sums, first_out, first_in,
    halves, second_out, second_in, blocks, last_keep, last_out, last_in,
    weight_sem, up_send, up_recv, dn_send, dn_recv, l_send, l_recv,
    core_send, core_recv, first_send, first_recv, second_send, second_recv, z_send, z_recv,
):
    features = x_ref.shape[1]
    wide = features // 4
    me = lax.axis_index("ffn")
    z = me // 8
    y = lax.rem(me // 4, 2)
    x = lax.rem(me // 2, 2)
    core = lax.rem(me, 2)
    mate = me + 1 - 2 * core
    xnbr = me + 2 - 4 * x
    ynbr = me + 4 - 8 * y

    loads = [
        pltpu.make_async_copy(src, dst, weight_sem.at[i])
        for i, (src, dst) in enumerate(((gate_hbm, gate_w), (up_hbm, up_w), (down_hbm, down_w)))
    ]
    for load in loads:
        load.start()

    def remote(src, dst, send, recv, target):
        return pltpu.make_async_remote_copy(
            src_ref=src, dst_ref=dst, send_sem=send, recv_sem=recv,
            device_id={"ffn": target}, device_id_type=MESH,
        )

    barrier = pltpu.get_barrier_semaphore()
    zpeers = [lax.rem(z + d, 4) * 8 + lax.rem(me, 8) for d in (1, 2, 3)]
    for partner in [mate, xnbr, ynbr] + zpeers:
        pl.semaphore_signal(barrier, inc=1, device_id={"ffn": partner}, device_id_type=MESH)

    row = lax.broadcasted_iota(jnp.int32, (16, LANES), 0)
    lane = lax.broadcasted_iota(jnp.int32, (16, LANES), 1)
    labels = jnp.zeros((16, LANES), F32)
    for t in range(4):
        for k, ref in enumerate((step_ref, segment_ref, code_ref)):
            labels = jnp.where((row == t) & (lane == k), ref[t].astype(F32), labels)

    def fold(ref):
        full = ref[...].astype(F32)
        return jnp.concatenate([full[:, c * wide:(c + 1) * wide] for c in range(4)], axis=0)

    raw[z, :, 0:LANES] = labels.astype(BF)
    raw[z, :, LANES:LANES + wide] = fold(x_ref).astype(BF)
    raw[z, :, LANES + wide:LANES + 2 * wide] = fold(g_ref).astype(BF)
    pl.semaphore_wait(barrier, 6)

    def upward(s, block):
        return remote(raw.at[block], raw.at[block], up_send.at[s], up_recv.at[s], me + 8)

    def downward(s, block):
        return remote(raw.at[block], raw.at[block], dn_send.at[s], dn_recv.at[s], me - 8)

    for s in range(3):
        @pl.when((z < 3) & (z - s >= 0))
        def _(s=s):
            upward(s, z - s).start()

        @pl.when((z > 0) & (z + s <= 3))
        def _(s=s):
            downward(s, z + s).start()

        @pl.when(z - 1 - s >= 0)
        def _(s=s):
            upward(s, z - 1 - s).wait_recv()

        @pl.when(z + 1 + s <= 3)
        def _(s=s):
            downward(s, z + 1 + s).wait_recv()

    mine = core * 4 + x * 2 + y
    by_y = core * 4 + x * 2 + 1 - y
    by_x = core * 4 + (1 - x) * 2 + y
    diag = core * 4 + (1 - x) * 2 + 1 - y
    flip = 4 - 8 * core
    xp = pl.ds(0, LANES + features)
    gp = pl.ds(LANES + features, features)

    pieces = [raw[k].astype(F32) for k in range(4)]
    rows[mine, :, 0:LANES] = jnp.concatenate(
        [piece[0:4, 0:LANES] for piece in pieces], axis=0
    ).astype(BF)
    for a in range(2):
        for c in range(4):
            lo = LANES + a * wide
            out = LANES + a * features + c * wide
            rows[mine, :, out:out + wide] = jnp.concatenate(
                [piece[4 * c:4 * c + 4, lo:lo + wide] for piece in pieces], axis=0
            ).astype(BF)

    def plane(i, block, columns, target):
        view = rows.at[block] if columns is None else rows.at[block, :, columns]
        return remote(view, view, l_send.at[i], l_recv.at[i], target)

    sends = [
        plane(0, mine, xp, ynbr),
        plane(1, mine, gp, xnbr),
        plane(2, mine, xp, xnbr),
        plane(3, mine, gp, ynbr),
        plane(4, mine, None, mate),
        plane(5, by_y, xp, xnbr),
        plane(6, by_x, gp, ynbr),
        plane(7, by_x, None, mate),
        plane(8, by_y, None, mate),
        plane(9, diag, None, mate),
    ]
    takes = [
        plane(0, by_y, xp, ynbr),
        plane(1, by_x, gp, xnbr),
        plane(2, by_x, xp, xnbr),
        plane(3, by_y, gp, ynbr),
        plane(4, mine + flip, None, mate),
        plane(5, diag, xp, xnbr),
        plane(6, diag, gp, ynbr),
        plane(7, by_x + flip, None, mate),
        plane(8, by_y + flip, None, mate),
        plane(9, diag + flip, None, mate),
    ]
    for i in range(5):
        sends[i].start()
    takes[0].wait_recv()
    sends[5].start()
    takes[1].wait_recv()
    sends[6].start()
    takes[2].wait_recv()
    sends[7].start()
    takes[3].wait_recv()
    sends[8].start()
    takes[5].wait_recv()
    takes[6].wait_recv()
    sends[9].start()
    for i in (4, 7, 8, 9):
        takes[i].wait_recv()

    tokens = 8 * 16
    tags = rows[:, :, 0:LANES].reshape(tokens, LANES)
    pick = (
        lax.broadcasted_iota(jnp.int32, (16, LANES), 0)
        == lax.broadcasted_iota(jnp.int32, (16, LANES), 1)
    ).astype(F32).astype(BF)
    across = contract_last(pick, tags)
    down = tags.astype(F32)
    gap = across[0:1, :] - down[:, 0:1]
    same = across[1:2, :] == down[:, 1:2]
    decay = jnp.where(same & (gap >= 0.0), jnp.exp(gap * math.log(0.75)), 0.0)
    total = jnp.sum(decay * across[2:3, :], axis=1, keepdims=True)
    count = jnp.sum(jnp.where(same, 1.0, 0.0), axis=1, keepdims=True)
    advantage = total / (8.0 * jnp.sqrt(count))

    for load in loads:
        load.wait()
    gate_pre = jnp.zeros((tokens, gate_w.shape[0]), F32)
    up_pre = jnp.zeros((tokens, gate_w.shape[0]), F32)
    hidden_grad = jnp.zeros((tokens, gate_w.shape[0]), F32)
    for c in range(4):
        cols = slice(c * wide, (c + 1) * wide)
        xs = rows[:, :, LANES + c * wide:LANES + (c + 1) * wide].reshape(tokens, wide)
        gate_pre += contract_last(xs, gate_w[:, cols])
        up_pre += contract_last(xs, up_w[:, cols])
        lo = LANES + features + c * wide
        gs = rows[:, :, lo:lo + wide].reshape(tokens, wide)
        weighted = (advantage * gs.astype(F32)).astype(BF)
        weighted_all[:, cols] = weighted
        hidden_grad += contract_last(weighted, down_w[:, cols])
    sigma = 1.0 / (1.0 + jnp.exp(-gate_pre))
    hidden = (gate_pre * sigma * up_pre).astype(BF)
    up_delta = (hidden_grad * gate_pre * sigma).astype(BF)
    gate_delta = (hidden_grad * up_pre * sigma * (1.0 + gate_pre * (1.0 - sigma))).astype(BF)

    for k in range(4):
        cols = slice(k * wide, (k + 1) * wide)
        share = jnp.dot(gate_delta, gate_w[:, cols], preferred_element_type=F32)
        share += jnp.dot(up_delta, up_w[:, cols], preferred_element_type=F32)
        part[k] = share.reshape(8, 16, wide)
        core_out[k] = part[k, pl.ds((1 - core) * 4, 4)].astype(BF)
        remote(core_out.at[k], core_in.at[k], core_send.at[k], core_recv.at[k], mate).start()

    def first(k):
        return remote(
            first_out.at[k], first_in.at[k], first_send.at[k], first_recv.at[k],
            xnbr if k % 2 == 0 else ynbr,
        )

    def second(k):
        return remote(
            second_out.at[k], second_in.at[k], second_send.at[k], second_recv.at[k],
            ynbr if k % 2 == 0 else xnbr,
        )

    def weight_grad(out, delta, by_tokens):
        for c in range(4):
            cols = slice(c * wide, (c + 1) * wide)
            out[:, cols] = contract_first(delta, by_tokens(c)).astype(BF)

    def inputs_of(c):
        return rows[:, :, LANES + c * wide:LANES + (c + 1) * wide].reshape(tokens, wide)

    weight_grad(gate_grad_ref, gate_delta, inputs_of)
    for k in range(4):
        remote(core_out.at[k], core_in.at[k], core_send.at[k], core_recv.at[k], mate).wait_recv()
        sums[k] = part[k, pl.ds(core * 4, 4)] + core_in[k].astype(F32)
        for j in range(2):
            other = (1 - x) * 2 + j if k % 2 == 0 else j * 2 + 1 - y
            first_out[k, j] = sums[k, other].astype(BF)
        first(k).start()
    weight_grad(up_grad_ref, up_delta, inputs_of)
    for k in range(4):
        first(k).wait_recv()
        for j in range(2):
            own = x * 2 + j if k % 2 == 0 else j * 2 + y
            halves[k, j] = sums[k, own] + first_in[k, j].astype(F32)
        side = y if k % 2 == 0 else x
        second_out[k] = halves[k, 1 - side].astype(BF)
        second(k).start()
    weight_grad(down_grad_ref, hidden, lambda c: weighted_all[:, c * wide:(c + 1) * wide])
    for k in range(4):
        second(k).wait_recv()
        side = y if k % 2 == 0 else x
        blocks[k] = halves[k, side] + second_in[k].astype(F32)
    stripes = [blocks[k] for k in range(4)]
    for zz in range(4):
        folded = jnp.concatenate([stripe[4 * zz:4 * zz + 4, :] for stripe in stripes], axis=0)
        last_keep[zz] = folded
        last_out[zz] = folded.astype(BF)

    def last(d):
        there = lax.rem(z + d, 4)
        return remote(
            last_out.at[there], last_in.at[d - 1], z_send.at[d - 1], z_recv.at[d - 1],
            there * 8 + lax.rem(me, 8),
        )

    for d in (1, 2, 3):
        last(d).start()
    for d in (1, 2, 3):
        last(d).wait_recv()
    final = last_keep[z] + last_in[0].astype(F32) + last_in[1].astype(F32) + last_in[2].astype(F32)
    for k in range(4):
        input_grad_ref[:, k * wide:(k + 1) * wide] = final[4 * k:4 * k + 4, :].astype(BF)

    for s in range(3):
        @pl.when((z < 3) & (z - s >= 0))
        def _(s=s):
            upward(s, z - s).wait_send()

        @pl.when((z > 0) & (z + s <= 3))
        def _(s=s):
            downward(s, z + s).wait_send()
    for send in sends:
        send.wait_send()
    for k in range(4):
        remote(core_out.at[k], core_in.at[k], core_send.at[k], core_recv.at[k], mate).wait_send()
        first(k).wait_send()
        second(k).wait_send()
    for d in (1, 2, 3):
        last(d).wait_send()


def fused(
    hidden_in, out_grad, step_ids, segment_ids, advantage_codes, gate_weight, up_weight, down_weight
):
    features, units = gate_weight.shape
    tokens = 32 * hidden_in.shape[0]
    wide = features // 4
    vmem = pl.BlockSpec(memory_space=pltpu.VMEM)
    smem = pl.BlockSpec(memory_space=pltpu.SMEM)
    hbm = pl.BlockSpec(memory_space=pltpu.HBM)
    dma = pltpu.SemaphoreType.DMA
    input_grad, gate_grad, up_grad, down_grad = pl.pallas_call(
        gather_kernel,
        out_shape=(
            jax.ShapeDtypeStruct(hidden_in.shape, BF),
            jax.ShapeDtypeStruct((units, features), BF),
            jax.ShapeDtypeStruct((units, features), BF),
            jax.ShapeDtypeStruct((units, features), BF),
        ),
        in_specs=[vmem, vmem, smem, smem, smem, hbm, hbm, hbm],
        out_specs=(vmem,) * 4,
        scratch_shapes=[
            pltpu.VMEM((units, features), BF),
            pltpu.VMEM((units, features), BF),
            pltpu.VMEM((units, features), BF),
            pltpu.VMEM((tokens, features), BF),
            pltpu.VMEM((4, 16, LANES + 2 * wide), BF),
            pltpu.VMEM((8, 16, LANES + 2 * features), BF),
            pltpu.VMEM((4, 8, 16, wide), F32),
            pltpu.VMEM((4, 4, 16, wide), BF),
            pltpu.VMEM((4, 4, 16, wide), BF),
            pltpu.VMEM((4, 4, 16, wide), F32),
            pltpu.VMEM((4, 2, 16, wide), BF),
            pltpu.VMEM((4, 2, 16, wide), BF),
            pltpu.VMEM((4, 2, 16, wide), F32),
            pltpu.VMEM((4, 16, wide), BF),
            pltpu.VMEM((4, 16, wide), BF),
            pltpu.VMEM((4, 16, wide), F32),
            pltpu.VMEM((4, 16, wide), F32),
            pltpu.VMEM((4, 16, wide), BF),
            pltpu.VMEM((3, 16, wide), BF),
            dma((3,)),
            dma((3,)), dma((3,)), dma((3,)), dma((3,)),
            dma((10,)), dma((10,)),
            dma((4,)), dma((4,)), dma((4,)), dma((4,)), dma((4,)), dma((4,)),
            dma((3,)), dma((3,)),
        ],
        compiler_params=pltpu.CompilerParams(
            collective_id=0, has_side_effects=True, vmem_limit_bytes=36 * 1024 * 1024
        ),
        cost_estimate=pl.CostEstimate(
            flops=10 * tokens * features * units, bytes_accessed=6 * features * units, transcendentals=0
        ),
        name="gather_and_sum",
    )(
        hidden_in, out_grad, step_ids, segment_ids, advantage_codes,
        gate_weight.T, up_weight.T, down_weight,
    )
    return (input_grad, gate_grad.T, up_grad.T, down_grad)


def local(
    hidden_in, out_grad, step_ids, segment_ids, advantage_codes, gate_weight, up_weight, down_weight
):
    inputs_all, grads_all = (
        lax.all_gather(hidden_in, "ffn", axis=0, tiled=True),
        lax.all_gather(out_grad, "ffn", axis=0, tiled=True),
    )
    labels = lax.all_gather(
        jnp.stack([step_ids, segment_ids, advantage_codes]), "ffn", axis=1, tiled=True
    )
    advantage = advantage_weights(labels[0], labels[1], labels[2])
    weighted = (advantage[:, None] * grads_all.astype(jnp.float32)).astype(jnp.bfloat16)
    gate_part = jnp.dot(inputs_all, gate_weight, preferred_element_type=jnp.float32)
    up_part = jnp.dot(inputs_all, up_weight, preferred_element_type=jnp.float32)
    gate_pre, up_pre = lax.psum((gate_part, up_part), "mp")
    sigma = jax.nn.sigmoid(gate_pre)
    hidden = (gate_pre * sigma * up_pre).astype(jnp.bfloat16)
    hidden_grad = lax.psum(contract_last(weighted, down_weight), "mp")
    up_delta = (hidden_grad * gate_pre * sigma).astype(jnp.bfloat16)
    gate_delta = (hidden_grad * up_pre * sigma * (1.0 + gate_pre * (1.0 - sigma))).astype(
        jnp.bfloat16
    )
    down_grad = contract_first(hidden, weighted).astype(jnp.bfloat16)
    gate_grad = contract_first(inputs_all, gate_delta).astype(jnp.bfloat16)
    up_grad = contract_first(inputs_all, up_delta).astype(jnp.bfloat16)
    partial_grad = contract_last(gate_delta, gate_weight) + contract_last(up_delta, up_weight)
    input_grad = lax.psum_scatter(partial_grad, "ffn", scatter_dimension=0, tiled=True)
    return (input_grad.astype(jnp.bfloat16), gate_grad, up_grad, down_grad)


def solution(mesh):
    in_specs = (
        P(("groups", "ffn"), "mp"),
        P(("groups", "ffn"), "mp"),
        P(("groups", "ffn")),
        P(("groups", "ffn")),
        P(("groups", "ffn")),
        P("mp", "ffn"),
        P("mp", "ffn"),
        P("ffn", "mp"),
    )
    out_specs = (
        P(("groups", "ffn"), "mp"),
        P(("groups", "mp"), "ffn"),
        P(("groups", "mp"), "ffn"),
        P(("groups", "ffn"), "mp"),
    )
    whole = mesh.shape["groups"] == 1 and mesh.shape["mp"] == 1 and mesh.shape["ffn"] == 32
    return jax.shard_map(fused if whole else local, mesh=mesh, in_specs=in_specs, out_specs=out_specs, check_vma=False)
```

```python
import math

import jax
import jax.numpy as jnp
from jax import lax
from jax.experimental import pallas as pl
from jax.experimental.pallas import tpu as pltpu
from jax.sharding import PartitionSpec as P


def advantage_weights(steps, segments, codes):
    same = segments[:, None] == segments[None, :]
    later = steps[None, :] >= steps[:, None]
    gap = (steps[None, :] - steps[:, None]).astype(jnp.float32)
    kernel = jnp.where(same & later, jnp.exp(gap * math.log(0.75)), jnp.zeros_like(gap))
    total = jnp.dot(kernel, codes.astype(jnp.float32), precision=lax.Precision.HIGHEST)
    count = jnp.sum(same.astype(jnp.float32), axis=1)
    return total / (8.0 * jnp.sqrt(count))


def contract_last(left, right):
    return lax.dot_general(
        left, right, (((1,), (1,)), ((), ())), preferred_element_type=jnp.float32
    )


def contract_first(left, right):
    return lax.dot_general(
        left, right, (((0,), (0,)), ((), ())), preferred_element_type=jnp.float32
    )


BF = jnp.bfloat16
F32 = jnp.float32
MESH = pl.DeviceIdType.MESH
LANES = 128


def gather_kernel(
    x_hbm, g_hbm, step_hbm, segment_hbm, code_hbm, gate_hbm, up_hbm, down_hbm,
    input_grad_ref, gate_grad_ref, up_grad_ref, down_grad_ref,
    gate_w, up_w, down_w, weighted_all, x_ref, g_ref, step_ref, segment_ref, code_ref,
    raw, rows, core_out, core_in, sums, first_out, first_in,
    halves, second_out, second_in, blocks, last_keep, last_out, last_in,
    load_sem, za_send, za_recv, x_send, x_recv, y_send, y_recv, fx_send, fx_recv, fy_send, fy_recv,
    m_send, m_recv,
    core_send, core_recv, first_send, first_recv, second_send, second_recv, z_send, z_recv,
):
    features = x_ref.shape[1]
    wide = features // 4
    tokens = 8 * 16
    me = lax.axis_index("ffn")
    z = me // 8
    y = lax.rem(me // 4, 2)
    x = lax.rem(me // 2, 2)
    core = lax.rem(me, 2)
    mate = me + 1 - 2 * core
    xnbr = me + 2 - 4 * x
    ynbr = me + 4 - 8 * y
    ahead = [me] + [lax.rem(z + d, 4) * 8 + lax.rem(me, 8) for d in (1, 2, 3)]
    behind = [me] + [lax.rem(z + 4 - d, 4) * 8 + lax.rem(me, 8) for d in (1, 2, 3)]

    loads = [
        pltpu.make_async_copy(src, dst, load_sem.at[i])
        for i, (src, dst) in enumerate((
            (x_hbm, x_ref), (g_hbm, g_ref), (step_hbm, step_ref), (segment_hbm, segment_ref),
            (code_hbm, code_ref), (gate_hbm, gate_w), (up_hbm, up_w), (down_hbm, down_w),
        ))
    ]
    for load in loads:
        load.start()

    def remote(src, dst, send, recv, target):
        return pltpu.make_async_remote_copy(
            src_ref=src, dst_ref=dst, send_sem=send, recv_sem=recv,
            device_id={"ffn": target}, device_id_type=MESH,
        )

    barrier = pltpu.get_barrier_semaphore()
    for partner in [mate, xnbr, ynbr] + ahead[1:]:
        pl.semaphore_signal(barrier, inc=1, device_id={"ffn": partner}, device_id_type=MESH)

    for load in loads[:5]:
        load.wait()
    row = lax.broadcasted_iota(jnp.int32, (16, LANES), 0)
    lane = lax.broadcasted_iota(jnp.int32, (16, LANES), 1)
    labels = jnp.zeros((16, LANES), F32)
    for t in range(4):
        for k, ref in enumerate((step_ref, segment_ref, code_ref)):
            labels = jnp.where((row == t) & (lane == k), ref[t].astype(F32), labels)

    def fold(ref):
        full = ref[...].astype(F32)
        return jnp.concatenate([full[:, c * wide:(c + 1) * wide] for c in range(4)], axis=0)

    raw[0, 0, :, 0:LANES] = labels.astype(BF)
    raw[0, 0, :, LANES:LANES + wide] = fold(x_ref).astype(BF)
    raw[0, 0, :, LANES + wide:LANES + 2 * wide] = fold(g_ref).astype(BF)
    pl.semaphore_wait(barrier, 6)

    xp = pl.ds(0, LANES + wide)
    gp = pl.ds(LANES + wide, wide)
    along_z = [
        remote(raw.at[0, 0], raw.at[0, d], za_send.at[d - 1], za_recv.at[d - 1], ahead[d])
        for d in (1, 2, 3)
    ]
    to_x = [remote(raw.at[0, d], raw.at[2, d], x_send.at[d], x_recv.at[d], xnbr) for d in range(4)]
    to_y = [remote(raw.at[0, d], raw.at[1, d], y_send.at[d], y_recv.at[d], ynbr) for d in range(4)]
    on_x = [
        remote(raw.at[1, d, :, xp], raw.at[3, d, :, xp], fx_send.at[d], fx_recv.at[d], xnbr)
        for d in range(4)
    ]
    on_y = [
        remote(raw.at[2, d, :, gp], raw.at[3, d, :, gp], fy_send.at[d], fy_recv.at[d], ynbr)
        for d in range(4)
    ]

    def to_mate(slot, half):
        pieces = pl.ds(2 * half, 2)
        i = 2 * slot + half
        return remote(
            raw.at[slot, pieces], raw.at[4 + slot, pieces], m_send.at[i], m_recv.at[i], mate
        )

    def onward(d):
        to_y[d].wait_recv()
        on_x[d].start()
        to_x[d].wait_recv()
        on_y[d].start()

    def unfold(slot):
        pieces = [raw[slot, d].astype(F32) for d in range(4)]
        rows[slot, :, 0:LANES] = jnp.concatenate(
            [piece[0:4, 0:LANES] for piece in pieces], axis=0
        ).astype(BF)
        for a in range(2):
            for c in range(4):
                lo = LANES + a * wide
                out = LANES + a * features + c * wide
                rows[slot, :, out:out + wide] = jnp.concatenate(
                    [piece[4 * c:4 * c + 4, lo:lo + wide] for piece in pieces], axis=0
                ).astype(BF)

    for copy in along_z:
        copy.start()
    to_y[0].start()
    to_x[0].start()
    for d in (1, 2, 3):
        along_z[d - 1].wait_recv()
        to_y[d].start()
        to_x[d].start()
        if d % 2 == 1:
            to_mate(0, d // 2).start()
        onward(d - 1)
        if d == 2:
            to_mate(1, 0).start()
            to_mate(2, 0).start()
    unfold(0)
    onward(3)
    to_mate(1, 1).start()
    to_mate(2, 1).start()
    for d in (0, 1):
        on_x[d].wait_recv()
        on_y[d].wait_recv()
    to_mate(3, 0).start()
    unfold(1)
    unfold(2)
    for d in (2, 3):
        on_x[d].wait_recv()
        on_y[d].wait_recv()
    to_mate(3, 1).start()
    unfold(3)
    for slot in range(4):
        to_mate(slot, 0).wait_recv()
        to_mate(slot, 1).wait_recv()
        unfold(4 + slot)

    tags = rows[:, :, 0:LANES].reshape(tokens, LANES)
    pick = (
        lax.broadcasted_iota(jnp.int32, (16, LANES), 0)
        == lax.broadcasted_iota(jnp.int32, (16, LANES), 1)
    ).astype(F32).astype(BF)
    across = contract_last(pick, tags)
    down = tags.astype(F32)
    gap = across[0:1, :] - down[:, 0:1]
    same = across[1:2, :] == down[:, 1:2]
    decay = jnp.where(same & (gap >= 0.0), jnp.exp(gap * math.log(0.75)), 0.0)
    total = jnp.sum(decay * across[2:3, :], axis=1, keepdims=True)
    count = jnp.sum(jnp.where(same, 1.0, 0.0), axis=1, keepdims=True)
    advantage = total / (8.0 * jnp.sqrt(count))

    for load in loads[5:]:
        load.wait()

    def inputs_of(c):
        return rows[:, :, LANES + c * wide:LANES + (c + 1) * wide].reshape(tokens, wide)

    gate_pre = jnp.zeros((tokens, gate_w.shape[0]), F32)
    up_pre = jnp.zeros((tokens, gate_w.shape[0]), F32)
    hidden_grad = jnp.zeros((tokens, gate_w.shape[0]), F32)
    for c in range(4):
        cols = slice(c * wide, (c + 1) * wide)
        xs = inputs_of(c)
        gate_pre += contract_last(xs, gate_w[:, cols])
        up_pre += contract_last(xs, up_w[:, cols])
        lo = LANES + features + c * wide
        gs = rows[:, :, lo:lo + wide].reshape(tokens, wide)
        weighted = (advantage * gs.astype(F32)).astype(BF)
        weighted_all[:, cols] = weighted
        hidden_grad += contract_last(weighted, down_w[:, cols])
    sigma = 1.0 / (1.0 + jnp.exp(-gate_pre))
    hidden = (gate_pre * sigma * up_pre).astype(BF)
    up_delta = (hidden_grad * gate_pre * sigma).astype(BF)
    gate_delta = (hidden_grad * up_pre * sigma * (1.0 + gate_pre * (1.0 - sigma))).astype(BF)

    to_core = [
        remote(core_out.at[k], core_in.at[k], core_send.at[k], core_recv.at[k], mate)
        for k in range(4)
    ]
    first = [
        remote(
            first_out.at[k], first_in.at[k], first_send.at[k], first_recv.at[k],
            xnbr if k % 2 == 0 else ynbr,
        )
        for k in range(4)
    ]
    second = [
        remote(
            second_out.at[k], second_in.at[k], second_send.at[k], second_recv.at[k],
            ynbr if k % 2 == 0 else xnbr,
        )
        for k in range(4)
    ]
    last = [
        remote(last_out.at[d - 1], last_in.at[d - 1], z_send.at[d - 1], z_recv.at[d - 1], behind[d])
        for d in (1, 2, 3)
    ]
    for k in range(4):
        cols = slice(k * wide, (k + 1) * wide)
        share = jnp.dot(gate_delta, gate_w[:, cols], preferred_element_type=F32)
        share += jnp.dot(up_delta, up_w[:, cols], preferred_element_type=F32)
        share = share.reshape(8, 16, wide)
        core_out[k] = share[4:8].astype(BF)
        to_core[k].start()
        sums[k] = share[0:4]

    def weight_grad(out, delta, by_tokens):
        for c in range(4):
            cols = slice(c * wide, (c + 1) * wide)
            out[:, cols] = contract_first(delta, by_tokens(c)).astype(BF)

    for k in range(4):
        leave, stay = ((2, 3), (0, 1)) if k % 2 == 0 else ((1, 3), (0, 2))
        to_core[k].wait_recv()
        for j in range(2):
            first_out[k, j] = (sums[k, leave[j]] + core_in[k, leave[j]].astype(F32)).astype(BF)
        first[k].start()
        for j in range(2):
            halves[k, j] = sums[k, stay[j]] + core_in[k, stay[j]].astype(F32)
    weight_grad(gate_grad_ref, gate_delta, inputs_of)
    for k in range(4):
        first[k].wait_recv()
        second_out[k] = (halves[k, 1] + first_in[k, 1].astype(F32)).astype(BF)
        second[k].start()
        blocks[k] = halves[k, 0] + first_in[k, 0].astype(F32)
    weight_grad(up_grad_ref, up_delta, inputs_of)
    for k in range(4):
        second[k].wait_recv()
    stripes = [blocks[k] + second_in[k].astype(F32) for k in range(4)]
    for d in (3, 2, 1, 0):
        folded = jnp.concatenate([stripe[4 * d:4 * d + 4, :] for stripe in stripes], axis=0)
        if d == 0:
            last_keep[...] = folded
        else:
            last_out[d - 1] = folded.astype(BF)
            last[d - 1].start()
    weight_grad(down_grad_ref, hidden, lambda c: weighted_all[:, c * wide:(c + 1) * wide])
    final = last_keep[...]
    for d in range(3):
        last[d].wait_recv()
        final += last_in[d].astype(F32)
    for k in range(4):
        input_grad_ref[:, k * wide:(k + 1) * wide] = final[4 * k:4 * k + 4, :].astype(BF)

    for copy in along_z + to_x + to_y + on_x + on_y:
        copy.wait_send()
    for slot in range(4):
        to_mate(slot, 0).wait_send()
        to_mate(slot, 1).wait_send()
    for copy in to_core + first + second + last:
        copy.wait_send()


def store_kernel(*refs):
    count = len(refs) // 2
    sources, targets, sems = refs[:count], refs[count:2 * count], refs[-1]
    copies = [
        pltpu.make_async_copy(src, dst, sems.at[i])
        for i, (src, dst) in enumerate(zip(sources, targets))
    ]
    for copy in copies:
        copy.start()
    for copy in copies:
        copy.wait()


def fused(
    hidden_in, out_grad, step_ids, segment_ids, advantage_codes, gate_weight, up_weight, down_weight
):
    features, units = gate_weight.shape
    local_tokens = hidden_in.shape[0]
    tokens = 32 * local_tokens
    wide = features // 4
    vmem = pl.BlockSpec(memory_space=pltpu.VMEM)
    hbm = pl.BlockSpec(memory_space=pl.ANY)
    dma = pltpu.SemaphoreType.DMA
    shapes = (
        jax.ShapeDtypeStruct(hidden_in.shape, BF),
        jax.ShapeDtypeStruct((units, features), BF),
        jax.ShapeDtypeStruct((units, features), BF),
        jax.ShapeDtypeStruct((units, features), BF),
    )
    grads = pl.pallas_call(
        gather_kernel,
        out_shape=shapes,
        in_specs=[hbm] * 8,
        out_specs=(vmem,) * 4,
        scratch_shapes=[
            pltpu.VMEM((units, features), BF),
            pltpu.VMEM((units, features), BF),
            pltpu.VMEM((units, features), BF),
            pltpu.VMEM((tokens, features), BF),
            pltpu.VMEM((local_tokens, features), BF),
            pltpu.VMEM((local_tokens, features), BF),
            pltpu.SMEM((local_tokens,), jnp.int32),
            pltpu.SMEM((local_tokens,), jnp.int32),
            pltpu.SMEM((local_tokens,), jnp.int32),
            pltpu.VMEM((8, 4, 16, LANES + 2 * wide), BF),
            pltpu.VMEM((8, 16, LANES + 2 * features), BF),
            pltpu.VMEM((4, 4, 16, wide), BF),
            pltpu.VMEM((4, 4, 16, wide), BF),
            pltpu.VMEM((4, 4, 16, wide), F32),
            pltpu.VMEM((4, 2, 16, wide), BF),
            pltpu.VMEM((4, 2, 16, wide), BF),
            pltpu.VMEM((4, 2, 16, wide), F32),
            pltpu.VMEM((4, 16, wide), BF),
            pltpu.VMEM((4, 16, wide), BF),
            pltpu.VMEM((4, 16, wide), F32),
            pltpu.VMEM((16, wide), F32),
            pltpu.VMEM((3, 16, wide), BF),
            pltpu.VMEM((3, 16, wide), BF),
            dma((8,)),
            dma((3,)), dma((3,)),
            dma((4,)), dma((4,)), dma((4,)), dma((4,)),
            dma((4,)), dma((4,)), dma((4,)), dma((4,)),
            dma((8,)), dma((8,)),
            dma((4,)), dma((4,)), dma((4,)), dma((4,)), dma((4,)), dma((4,)),
            dma((3,)), dma((3,)),
        ],
        compiler_params=pltpu.CompilerParams(
            collective_id=0, has_side_effects=True, vmem_limit_bytes=36 * 1024 * 1024
        ),
        name="gather_and_sum",
    )(*[
        pltpu.with_memory_space_constraint(value, pltpu.HBM)
        for value in (
            hidden_in, out_grad, step_ids, segment_ids, advantage_codes,
            gate_weight.T, up_weight.T, down_weight,
        )
    ])
    input_grad, gate_grad, up_grad, down_grad = pl.pallas_call(
        store_kernel,
        out_shape=shapes,
        in_specs=[hbm] * 4,
        out_specs=(hbm,) * 4,
        scratch_shapes=[dma((4,))],
        name="store",
    )(*grads)
    return (input_grad, gate_grad.T, up_grad.T, down_grad)


def local(
    hidden_in, out_grad, step_ids, segment_ids, advantage_codes, gate_weight, up_weight, down_weight
):
    inputs_all, grads_all = (
        lax.all_gather(hidden_in, "ffn", axis=0, tiled=True),
        lax.all_gather(out_grad, "ffn", axis=0, tiled=True),
    )
    labels = lax.all_gather(
        jnp.stack([step_ids, segment_ids, advantage_codes]), "ffn", axis=1, tiled=True
    )
    advantage = advantage_weights(labels[0], labels[1], labels[2])
    weighted = (advantage[:, None] * grads_all.astype(jnp.float32)).astype(jnp.bfloat16)
    gate_part = jnp.dot(inputs_all, gate_weight, preferred_element_type=jnp.float32)
    up_part = jnp.dot(inputs_all, up_weight, preferred_element_type=jnp.float32)
    gate_pre, up_pre = lax.psum((gate_part, up_part), "mp")
    sigma = jax.nn.sigmoid(gate_pre)
    hidden = (gate_pre * sigma * up_pre).astype(jnp.bfloat16)
    hidden_grad = lax.psum(contract_last(weighted, down_weight), "mp")
    up_delta = (hidden_grad * gate_pre * sigma).astype(jnp.bfloat16)
    gate_delta = (hidden_grad * up_pre * sigma * (1.0 + gate_pre * (1.0 - sigma))).astype(
        jnp.bfloat16
    )
    down_grad = contract_first(hidden, weighted).astype(jnp.bfloat16)
    gate_grad = contract_first(inputs_all, gate_delta).astype(jnp.bfloat16)
    up_grad = contract_first(inputs_all, up_delta).astype(jnp.bfloat16)
    partial_grad = contract_last(gate_delta, gate_weight) + contract_last(up_delta, up_weight)
    input_grad = lax.psum_scatter(partial_grad, "ffn", scatter_dimension=0, tiled=True)
    return (input_grad.astype(jnp.bfloat16), gate_grad, up_grad, down_grad)


def solution(mesh):
    in_specs = (
        P(("groups", "ffn"), "mp"),
        P(("groups", "ffn"), "mp"),
        P(("groups", "ffn")),
        P(("groups", "ffn")),
        P(("groups", "ffn")),
        P("mp", "ffn"),
        P("mp", "ffn"),
        P("ffn", "mp"),
    )
    out_specs = (
        P(("groups", "ffn"), "mp"),
        P(("groups", "mp"), "ffn"),
        P(("groups", "mp"), "ffn"),
        P(("groups", "ffn"), "mp"),
    )
    whole = mesh.shape["groups"] == 1 and mesh.shape["mp"] == 1 and mesh.shape["ffn"] == 32
    return jax.shard_map(fused if whole else local, mesh=mesh, in_specs=in_specs, out_specs=out_specs, check_vma=False)
```

```python
import math

import jax
import jax.numpy as jnp
from jax import lax
from jax.experimental import pallas as pl
from jax.experimental.pallas import tpu as pltpu
from jax.sharding import PartitionSpec as P


def advantage_weights(steps, segments, codes):
    same = segments[:, None] == segments[None, :]
    later = steps[None, :] >= steps[:, None]
    gap = (steps[None, :] - steps[:, None]).astype(jnp.float32)
    kernel = jnp.where(same & later, jnp.exp(gap * math.log(0.75)), jnp.zeros_like(gap))
    total = jnp.dot(kernel, codes.astype(jnp.float32), precision=lax.Precision.HIGHEST)
    count = jnp.sum(same.astype(jnp.float32), axis=1)
    return total / (8.0 * jnp.sqrt(count))


def contract_last(left, right):
    return lax.dot_general(
        left, right, (((1,), (1,)), ((), ())), preferred_element_type=jnp.float32
    )


def contract_first(left, right):
    return lax.dot_general(
        left, right, (((0,), (0,)), ((), ())), preferred_element_type=jnp.float32
    )


BF = jnp.bfloat16
F32 = jnp.float32
MESH = pl.DeviceIdType.MESH
LANES = 128


def gather_kernel(
    x_hbm, g_hbm, step_hbm, segment_hbm, code_hbm, gate_hbm, up_hbm, down_hbm,
    input_grad_ref, gate_grad_ref, up_grad_ref, down_grad_ref,
    gate_w, up_w, down_w, weighted_all, x_ref, g_ref, step_ref, segment_ref, code_ref,
    raw, rows, core_out, core_in, sums, first_out, first_in,
    halves, second_out, second_in, blocks, last_keep, last_out, last_in,
    load_sem, za_send, za_recv, x_send, x_recv, y_send, y_recv, fx_send, fx_recv, fy_send, fy_recv,
    m_send, m_recv,
    core_send, core_recv, first_send, first_recv, second_send, second_recv, z_send, z_recv,
):
    features = x_ref.shape[1]
    wide = features // 4
    tokens = 8 * 16
    me = lax.axis_index("ffn")
    z = me // 8
    y = lax.rem(me // 4, 2)
    x = lax.rem(me // 2, 2)
    core = lax.rem(me, 2)
    mate = me + 1 - 2 * core
    xnbr = me + 2 - 4 * x
    ynbr = me + 4 - 8 * y
    ahead = [me] + [lax.rem(z + d, 4) * 8 + lax.rem(me, 8) for d in (1, 2, 3)]
    behind = [me] + [lax.rem(z + 4 - d, 4) * 8 + lax.rem(me, 8) for d in (1, 2, 3)]

    loads = [
        pltpu.make_async_copy(src, dst, load_sem.at[i])
        for i, (src, dst) in enumerate((
            (x_hbm, x_ref), (g_hbm, g_ref), (step_hbm, step_ref), (segment_hbm, segment_ref),
            (code_hbm, code_ref), (gate_hbm, gate_w), (up_hbm, up_w), (down_hbm, down_w),
        ))
    ]
    for load in loads:
        load.start()

    def remote(src, dst, send, recv, target):
        return pltpu.make_async_remote_copy(
            src_ref=src, dst_ref=dst, send_sem=send, recv_sem=recv,
            device_id={"ffn": target}, device_id_type=MESH,
        )

    barrier = pltpu.get_barrier_semaphore()
    for partner in [mate, xnbr, ynbr] + ahead[1:]:
        pl.semaphore_signal(barrier, inc=1, device_id={"ffn": partner}, device_id_type=MESH)

    for load in loads[:5]:
        load.wait()
    row = lax.broadcasted_iota(jnp.int32, (16, LANES), 0)
    lane = lax.broadcasted_iota(jnp.int32, (16, LANES), 1)
    labels = jnp.zeros((16, LANES), F32)
    for t in range(4):
        for k, ref in enumerate((step_ref, segment_ref, code_ref)):
            labels = jnp.where((row == t) & (lane == k), ref[t].astype(F32), labels)

    def fold(ref):
        full = ref[...].astype(F32)
        return jnp.concatenate([full[:, c * wide:(c + 1) * wide] for c in range(4)], axis=0)

    raw[0, 0, :, 0:LANES] = labels.astype(BF)
    raw[0, 0, :, LANES:LANES + wide] = fold(x_ref).astype(BF)
    raw[0, 0, :, LANES + wide:LANES + 2 * wide] = fold(g_ref).astype(BF)
    pl.semaphore_wait(barrier, 6)

    xp = pl.ds(0, LANES + wide)
    gp = pl.ds(LANES + wide, wide)
    along_z = [
        remote(raw.at[0, 0], raw.at[0, d], za_send.at[d - 1], za_recv.at[d - 1], ahead[d])
        for d in (1, 2, 3)
    ]
    to_x = [remote(raw.at[0, d], raw.at[2, d], x_send.at[d], x_recv.at[d], xnbr) for d in range(4)]
    to_y = [remote(raw.at[0, d], raw.at[1, d], y_send.at[d], y_recv.at[d], ynbr) for d in range(4)]
    on_x = [
        remote(raw.at[1, d, :, xp], raw.at[3, d, :, xp], fx_send.at[d], fx_recv.at[d], xnbr)
        for d in range(4)
    ]
    on_y = [
        remote(raw.at[2, d, :, gp], raw.at[3, d, :, gp], fy_send.at[d], fy_recv.at[d], ynbr)
        for d in range(4)
    ]

    def to_mate(slot, half):
        pieces = pl.ds(2 * half, 2)
        i = 2 * slot + half
        return remote(
            raw.at[slot, pieces], raw.at[4 + slot, pieces], m_send.at[i], m_recv.at[i], mate
        )

    def onward(d):
        to_y[d].wait_recv()
        on_x[d].start()
        to_x[d].wait_recv()
        on_y[d].start()

    def unfold(slot):
        pieces = [raw[slot, d].astype(F32) for d in range(4)]
        rows[slot, :, 0:LANES] = jnp.concatenate(
            [piece[0:4, 0:LANES] for piece in pieces], axis=0
        ).astype(BF)
        for a in range(2):
            for c in range(4):
                lo = LANES + a * wide
                out = LANES + a * features + c * wide
                rows[slot, :, out:out + wide] = jnp.concatenate(
                    [piece[4 * c:4 * c + 4, lo:lo + wide] for piece in pieces], axis=0
                ).astype(BF)

    for copy in along_z:
        copy.start()
    to_y[0].start()
    to_x[0].start()
    for d in (1, 2, 3):
        along_z[d - 1].wait_recv()
        to_y[d].start()
        to_x[d].start()
        if d % 2 == 1:
            to_mate(0, d // 2).start()
        onward(d - 1)
        if d == 2:
            to_mate(1, 0).start()
            to_mate(2, 0).start()
    unfold(0)
    onward(3)
    to_mate(1, 1).start()
    to_mate(2, 1).start()
    for d in (0, 1):
        on_x[d].wait_recv()
        on_y[d].wait_recv()
    to_mate(3, 0).start()
    unfold(1)
    unfold(2)
    for d in (2, 3):
        on_x[d].wait_recv()
        on_y[d].wait_recv()
    to_mate(3, 1).start()
    unfold(3)
    for slot in range(4):
        to_mate(slot, 0).wait_recv()
        to_mate(slot, 1).wait_recv()
        unfold(4 + slot)

    tags = rows[:, :, 0:LANES].reshape(tokens, LANES)
    pick = (
        lax.broadcasted_iota(jnp.int32, (16, LANES), 0)
        == lax.broadcasted_iota(jnp.int32, (16, LANES), 1)
    ).astype(F32).astype(BF)
    across = contract_last(pick, tags)
    down = tags.astype(F32)
    gap = across[0:1, :] - down[:, 0:1]
    same = across[1:2, :] == down[:, 1:2]
    decay = jnp.where(same & (gap >= 0.0), jnp.exp(gap * math.log(0.75)), 0.0)
    total = jnp.sum(decay * across[2:3, :], axis=1, keepdims=True)
    count = jnp.sum(jnp.where(same, 1.0, 0.0), axis=1, keepdims=True)
    advantage = total / (8.0 * jnp.sqrt(count))

    for load in loads[5:]:
        load.wait()

    def inputs_of(c):
        return rows[:, :, LANES + c * wide:LANES + (c + 1) * wide].reshape(tokens, wide)

    gate_pre = jnp.zeros((tokens, gate_w.shape[0]), F32)
    up_pre = jnp.zeros((tokens, gate_w.shape[0]), F32)
    hidden_grad = jnp.zeros((tokens, gate_w.shape[0]), F32)
    for c in range(4):
        cols = slice(c * wide, (c + 1) * wide)
        xs = inputs_of(c)
        gate_pre += contract_last(xs, gate_w[:, cols])
        up_pre += contract_last(xs, up_w[:, cols])
        lo = LANES + features + c * wide
        gs = rows[:, :, lo:lo + wide].reshape(tokens, wide)
        weighted = (advantage * gs.astype(F32)).astype(BF)
        weighted_all[:, cols] = weighted
        hidden_grad += contract_last(weighted, down_w[:, cols])
    sigma = 1.0 / (1.0 + jnp.exp(-gate_pre))
    hidden = (gate_pre * sigma * up_pre).astype(BF)
    up_delta = (hidden_grad * gate_pre * sigma).astype(BF)
    gate_delta = (hidden_grad * up_pre * sigma * (1.0 + gate_pre * (1.0 - sigma))).astype(BF)

    to_core = [
        remote(core_out.at[k], core_in.at[k], core_send.at[k], core_recv.at[k], mate)
        for k in range(4)
    ]
    first = [
        remote(
            first_out.at[k], first_in.at[k], first_send.at[k], first_recv.at[k],
            xnbr if k % 2 == 0 else ynbr,
        )
        for k in range(4)
    ]
    second = [
        remote(
            second_out.at[k], second_in.at[k], second_send.at[k], second_recv.at[k],
            ynbr if k % 2 == 0 else xnbr,
        )
        for k in range(4)
    ]
    last = [
        remote(last_out.at[d - 1], last_in.at[d - 1], z_send.at[d - 1], z_recv.at[d - 1], behind[d])
        for d in (1, 2, 3)
    ]
    for k in range(4):
        cols = slice(k * wide, (k + 1) * wide)
        share = jnp.dot(gate_delta, gate_w[:, cols], preferred_element_type=F32)
        share += jnp.dot(up_delta, up_w[:, cols], preferred_element_type=F32)
        share = share.reshape(8, 16, wide)
        core_out[k] = share[4:8].astype(BF)
        to_core[k].start()
        sums[k] = share[0:4]

    def weight_grad(out, delta, by_tokens):
        for c in range(4):
            cols = slice(c * wide, (c + 1) * wide)
            out[:, cols] = contract_first(delta, by_tokens(c)).astype(BF)

    for k in range(4):
        leave, stay = ((2, 3), (0, 1)) if k % 2 == 0 else ((1, 3), (0, 2))
        to_core[k].wait_recv()
        for j in range(2):
            first_out[k, j] = (sums[k, leave[j]] + core_in[k, leave[j]].astype(F32)).astype(BF)
        first[k].start()
        for j in range(2):
            halves[k, j] = sums[k, stay[j]] + core_in[k, stay[j]].astype(F32)
    weight_grad(gate_grad_ref, gate_delta, inputs_of)
    for k in range(4):
        first[k].wait_recv()
        second_out[k] = (halves[k, 1] + first_in[k, 1].astype(F32)).astype(BF)
        second[k].start()
        blocks[k] = halves[k, 0] + first_in[k, 0].astype(F32)
    weight_grad(up_grad_ref, up_delta, inputs_of)
    for k in range(4):
        second[k].wait_recv()
    stripes = [blocks[k] + second_in[k].astype(F32) for k in range(4)]
    for d in (3, 2, 1, 0):
        folded = jnp.concatenate([stripe[4 * d:4 * d + 4, :] for stripe in stripes], axis=0)
        if d == 0:
            last_keep[...] = folded
        else:
            last_out[d - 1] = folded.astype(BF)
            last[d - 1].start()
    weight_grad(down_grad_ref, hidden, lambda c: weighted_all[:, c * wide:(c + 1) * wide])
    final = last_keep[...]
    for d in range(3):
        last[d].wait_recv()
        final += last_in[d].astype(F32)
    for k in range(4):
        input_grad_ref[:, k * wide:(k + 1) * wide] = final[4 * k:4 * k + 4, :].astype(BF)

    for copy in along_z + to_x + to_y + on_x + on_y:
        copy.wait_send()
    for slot in range(4):
        to_mate(slot, 0).wait_send()
        to_mate(slot, 1).wait_send()
    for copy in to_core + first + second + last:
        copy.wait_send()


def fused(
    hidden_in, out_grad, step_ids, segment_ids, advantage_codes, gate_weight, up_weight, down_weight
):
    features, units = gate_weight.shape
    local_tokens = hidden_in.shape[0]
    tokens = 32 * local_tokens
    wide = features // 4
    vmem = pl.BlockSpec(memory_space=pltpu.VMEM)
    hbm = pl.BlockSpec(memory_space=pl.ANY)
    dma = pltpu.SemaphoreType.DMA
    shapes = (
        jax.ShapeDtypeStruct(hidden_in.shape, BF),
        jax.ShapeDtypeStruct((units, features), BF),
        jax.ShapeDtypeStruct((units, features), BF),
        jax.ShapeDtypeStruct((units, features), BF),
    )
    input_grad, gate_grad, up_grad, down_grad = pl.pallas_call(
        gather_kernel,
        out_shape=shapes,
        in_specs=[hbm] * 8,
        out_specs=(vmem,) * 4,
        scratch_shapes=[
            pltpu.VMEM((units, features), BF),
            pltpu.VMEM((units, features), BF),
            pltpu.VMEM((units, features), BF),
            pltpu.VMEM((tokens, features), BF),
            pltpu.VMEM((local_tokens, features), BF),
            pltpu.VMEM((local_tokens, features), BF),
            pltpu.SMEM((local_tokens,), jnp.int32),
            pltpu.SMEM((local_tokens,), jnp.int32),
            pltpu.SMEM((local_tokens,), jnp.int32),
            pltpu.VMEM((8, 4, 16, LANES + 2 * wide), BF),
            pltpu.VMEM((8, 16, LANES + 2 * features), BF),
            pltpu.VMEM((4, 4, 16, wide), BF),
            pltpu.VMEM((4, 4, 16, wide), BF),
            pltpu.VMEM((4, 4, 16, wide), F32),
            pltpu.VMEM((4, 2, 16, wide), BF),
            pltpu.VMEM((4, 2, 16, wide), BF),
            pltpu.VMEM((4, 2, 16, wide), F32),
            pltpu.VMEM((4, 16, wide), BF),
            pltpu.VMEM((4, 16, wide), BF),
            pltpu.VMEM((4, 16, wide), F32),
            pltpu.VMEM((16, wide), F32),
            pltpu.VMEM((3, 16, wide), BF),
            pltpu.VMEM((3, 16, wide), BF),
            dma((8,)),
            dma((3,)), dma((3,)),
            dma((4,)), dma((4,)), dma((4,)), dma((4,)),
            dma((4,)), dma((4,)), dma((4,)), dma((4,)),
            dma((8,)), dma((8,)),
            dma((4,)), dma((4,)), dma((4,)), dma((4,)), dma((4,)), dma((4,)),
            dma((3,)), dma((3,)),
        ],
        compiler_params=pltpu.CompilerParams(
            collective_id=0, has_side_effects=True, vmem_limit_bytes=36 * 1024 * 1024
        ),
        name="gather_and_sum",
    )(*[
        pltpu.with_memory_space_constraint(value, pltpu.HBM)
        for value in (
            hidden_in, out_grad, step_ids, segment_ids, advantage_codes,
            gate_weight.T, up_weight.T, down_weight,
        )
    ])
    return (input_grad, gate_grad.T, up_grad.T, down_grad)


def local(
    hidden_in, out_grad, step_ids, segment_ids, advantage_codes, gate_weight, up_weight, down_weight
):
    inputs_all, grads_all = (
        lax.all_gather(hidden_in, "ffn", axis=0, tiled=True),
        lax.all_gather(out_grad, "ffn", axis=0, tiled=True),
    )
    labels = lax.all_gather(
        jnp.stack([step_ids, segment_ids, advantage_codes]), "ffn", axis=1, tiled=True
    )
    advantage = advantage_weights(labels[0], labels[1], labels[2])
    weighted = (advantage[:, None] * grads_all.astype(jnp.float32)).astype(jnp.bfloat16)
    gate_part = jnp.dot(inputs_all, gate_weight, preferred_element_type=jnp.float32)
    up_part = jnp.dot(inputs_all, up_weight, preferred_element_type=jnp.float32)
    gate_pre, up_pre = lax.psum((gate_part, up_part), "mp")
    sigma = jax.nn.sigmoid(gate_pre)
    hidden = (gate_pre * sigma * up_pre).astype(jnp.bfloat16)
    hidden_grad = lax.psum(contract_last(weighted, down_weight), "mp")
    up_delta = (hidden_grad * gate_pre * sigma).astype(jnp.bfloat16)
    gate_delta = (hidden_grad * up_pre * sigma * (1.0 + gate_pre * (1.0 - sigma))).astype(
        jnp.bfloat16
    )
    down_grad = contract_first(hidden, weighted).astype(jnp.bfloat16)
    gate_grad = contract_first(inputs_all, gate_delta).astype(jnp.bfloat16)
    up_grad = contract_first(inputs_all, up_delta).astype(jnp.bfloat16)
    partial_grad = contract_last(gate_delta, gate_weight) + contract_last(up_delta, up_weight)
    input_grad = lax.psum_scatter(partial_grad, "ffn", scatter_dimension=0, tiled=True)
    return (input_grad.astype(jnp.bfloat16), gate_grad, up_grad, down_grad)


def solution(mesh):
    in_specs = (
        P(("groups", "ffn"), "mp"),
        P(("groups", "ffn"), "mp"),
        P(("groups", "ffn")),
        P(("groups", "ffn")),
        P(("groups", "ffn")),
        P("mp", "ffn"),
        P("mp", "ffn"),
        P("ffn", "mp"),
    )
    out_specs = (
        P(("groups", "ffn"), "mp"),
        P(("groups", "mp"), "ffn"),
        P(("groups", "mp"), "ffn"),
        P(("groups", "ffn"), "mp"),
    )
    whole = mesh.shape["groups"] == 1 and mesh.shape["mp"] == 1 and mesh.shape["ffn"] == 32
    return jax.shard_map(fused if whole else local, mesh=mesh, in_specs=in_specs, out_specs=out_specs, check_vma=False)
```

```python
import math

import jax
import jax.numpy as jnp
from jax import lax
from jax.experimental import pallas as pl
from jax.experimental.pallas import tpu as pltpu
from jax.sharding import PartitionSpec as P


def advantage_weights(steps, segments, codes):
    same = segments[:, None] == segments[None, :]
    later = steps[None, :] >= steps[:, None]
    gap = (steps[None, :] - steps[:, None]).astype(jnp.float32)
    kernel = jnp.where(same & later, jnp.exp(gap * math.log(0.75)), jnp.zeros_like(gap))
    total = jnp.dot(kernel, codes.astype(jnp.float32), precision=lax.Precision.HIGHEST)
    count = jnp.sum(same.astype(jnp.float32), axis=1)
    return total / (8.0 * jnp.sqrt(count))


def contract_last(left, right):
    return lax.dot_general(
        left, right, (((1,), (1,)), ((), ())), preferred_element_type=jnp.float32
    )


def contract_first(left, right):
    return lax.dot_general(
        left, right, (((0,), (0,)), ((), ())), preferred_element_type=jnp.float32
    )


BF = jnp.bfloat16
F32 = jnp.float32
MESH = pl.DeviceIdType.MESH
LANES = 128


def gather_kernel(
    x_hbm, g_hbm, step_hbm, segment_hbm, code_hbm, gate_hbm, up_hbm, down_hbm,
    input_grad_ref, gate_grad_ref, up_grad_ref, down_grad_ref,
    gate_w, up_w, down_w, weighted_all, x_ref, g_ref, step_ref, segment_ref, code_ref,
    raw, rows, core_out, core_in, sums, first_out, first_in,
    halves, second_out, second_in, blocks, last_keep, last_out, last_in,
    load_sem, za_send, za_recv, x_send, x_recv, y_send, y_recv, d_send, d_recv,
    m_send, m_recv,
    core_send, core_recv, first_send, first_recv, second_send, second_recv, z_send, z_recv,
):
    features = x_ref.shape[1]
    wide = features // 4
    tokens = 8 * 16
    me = lax.axis_index("ffn")
    z = me // 8
    y = lax.rem(me // 4, 2)
    x = lax.rem(me // 2, 2)
    core = lax.rem(me, 2)
    mate = me + 1 - 2 * core
    xnbr = me + 2 - 4 * x
    ynbr = me + 4 - 8 * y
    across_xy = xnbr + 4 - 8 * y
    ahead = [me] + [lax.rem(z + d, 4) * 8 + lax.rem(me, 8) for d in (1, 2, 3)]
    behind = [me] + [lax.rem(z + 4 - d, 4) * 8 + lax.rem(me, 8) for d in (1, 2, 3)]

    loads = [
        pltpu.make_async_copy(src, dst, load_sem.at[i])
        for i, (src, dst) in enumerate((
            (x_hbm, x_ref), (g_hbm, g_ref), (step_hbm, step_ref), (segment_hbm, segment_ref),
            (code_hbm, code_ref), (gate_hbm, gate_w), (up_hbm, up_w), (down_hbm, down_w),
        ))
    ]
    for load in loads:
        load.start()

    def remote(src, dst, send, recv, target):
        return pltpu.make_async_remote_copy(
            src_ref=src, dst_ref=dst, send_sem=send, recv_sem=recv,
            device_id={"ffn": target}, device_id_type=MESH,
        )

    barrier = pltpu.get_barrier_semaphore()
    for partner in [mate, xnbr, ynbr, across_xy] + ahead[1:]:
        pl.semaphore_signal(barrier, inc=1, device_id={"ffn": partner}, device_id_type=MESH)

    for load in loads[:5]:
        load.wait()
    row = lax.broadcasted_iota(jnp.int32, (16, LANES), 0)
    lane = lax.broadcasted_iota(jnp.int32, (16, LANES), 1)
    labels = jnp.zeros((16, LANES), F32)
    for t in range(4):
        for k, ref in enumerate((step_ref, segment_ref, code_ref)):
            labels = jnp.where((row == t) & (lane == k), ref[t].astype(F32), labels)

    def fold(ref):
        full = ref[...].astype(F32)
        return jnp.concatenate([full[:, c * wide:(c + 1) * wide] for c in range(4)], axis=0)

    raw[0, 0, :, 0:LANES] = labels.astype(BF)
    raw[0, 0, :, LANES:LANES + wide] = fold(x_ref).astype(BF)
    raw[0, 0, :, LANES + wide:LANES + 2 * wide] = fold(g_ref).astype(BF)
    pl.semaphore_wait(barrier, 7)

    along_z = [
        remote(raw.at[0, 0], raw.at[0, d], za_send.at[d - 1], za_recv.at[d - 1], ahead[d])
        for d in (1, 2, 3)
    ]
    to_x = [remote(raw.at[0, d], raw.at[2, d], x_send.at[d], x_recv.at[d], xnbr) for d in range(4)]
    to_y = [remote(raw.at[0, d], raw.at[1, d], y_send.at[d], y_recv.at[d], ynbr) for d in range(4)]
    to_d = [remote(raw.at[0, d], raw.at[3, d], d_send.at[d], d_recv.at[d], across_xy) for d in range(4)]

    def to_mate(slot, half):
        pieces = pl.ds(2 * half, 2)
        i = 2 * slot + half
        return remote(
            raw.at[slot, pieces], raw.at[4 + slot, pieces], m_send.at[i], m_recv.at[i], mate
        )

    def unfold(slot):
        pieces = [raw[slot, d].astype(F32) for d in range(4)]
        rows[slot, :, 0:LANES] = jnp.concatenate(
            [piece[0:4, 0:LANES] for piece in pieces], axis=0
        ).astype(BF)
        for a in range(2):
            for c in range(4):
                lo = LANES + a * wide
                out = LANES + a * features + c * wide
                rows[slot, :, out:out + wide] = jnp.concatenate(
                    [piece[4 * c:4 * c + 4, lo:lo + wide] for piece in pieces], axis=0
                ).astype(BF)

    def spread(d):
        to_d[d].start()
        to_y[d].start()
        to_x[d].start()

    def arrive(half):
        for copies, slot in ((to_y, 1), (to_x, 2), (to_d, 3)):
            for d in (2 * half, 2 * half + 1):
                copies[d].wait_recv()
            to_mate(slot, half).start()

    for copy in along_z:
        copy.start()
    spread(0)
    for d in (1, 2, 3):
        along_z[d - 1].wait_recv()
        spread(d)
        if d % 2 == 1:
            to_mate(0, d // 2).start()
    unfold(0)
    arrive(0)
    arrive(1)
    for slot in (1, 2, 3):
        unfold(slot)
    for slot in range(4):
        to_mate(slot, 0).wait_recv()
        to_mate(slot, 1).wait_recv()
        unfold(4 + slot)

    tags = rows[:, :, 0:LANES].reshape(tokens, LANES)
    pick = (
        lax.broadcasted_iota(jnp.int32, (16, LANES), 0)
        == lax.broadcasted_iota(jnp.int32, (16, LANES), 1)
    ).astype(F32).astype(BF)
    across = contract_last(pick, tags)
    down = tags.astype(F32)
    gap = across[0:1, :] - down[:, 0:1]
    same = across[1:2, :] == down[:, 1:2]
    decay = jnp.where(same & (gap >= 0.0), jnp.exp(gap * math.log(0.75)), 0.0)
    total = jnp.sum(decay * across[2:3, :], axis=1, keepdims=True)
    count = jnp.sum(jnp.where(same, 1.0, 0.0), axis=1, keepdims=True)
    advantage = total / (8.0 * jnp.sqrt(count))

    for load in loads[5:]:
        load.wait()

    def inputs_of(c):
        return rows[:, :, LANES + c * wide:LANES + (c + 1) * wide].reshape(tokens, wide)

    gate_pre = jnp.zeros((tokens, gate_w.shape[0]), F32)
    up_pre = jnp.zeros((tokens, gate_w.shape[0]), F32)
    hidden_grad = jnp.zeros((tokens, gate_w.shape[0]), F32)
    for c in range(4):
        cols = slice(c * wide, (c + 1) * wide)
        xs = inputs_of(c)
        gate_pre += contract_last(xs, gate_w[:, cols])
        up_pre += contract_last(xs, up_w[:, cols])
        lo = LANES + features + c * wide
        gs = rows[:, :, lo:lo + wide].reshape(tokens, wide)
        weighted = (advantage * gs.astype(F32)).astype(BF)
        weighted_all[:, cols] = weighted
        hidden_grad += contract_last(weighted, down_w[:, cols])
    sigma = 1.0 / (1.0 + jnp.exp(-gate_pre))
    hidden = (gate_pre * sigma * up_pre).astype(BF)
    up_delta = (hidden_grad * gate_pre * sigma).astype(BF)
    gate_delta = (hidden_grad * up_pre * sigma * (1.0 + gate_pre * (1.0 - sigma))).astype(BF)

    to_core = [
        remote(core_out.at[k], core_in.at[k], core_send.at[k], core_recv.at[k], mate)
        for k in range(4)
    ]
    first = [
        remote(
            first_out.at[k], first_in.at[k], first_send.at[k], first_recv.at[k],
            xnbr if k % 2 == 0 else ynbr,
        )
        for k in range(4)
    ]
    second = [
        remote(
            second_out.at[k], second_in.at[k], second_send.at[k], second_recv.at[k],
            ynbr if k % 2 == 0 else xnbr,
        )
        for k in range(4)
    ]
    last = [
        remote(last_out.at[d - 1], last_in.at[d - 1], z_send.at[d - 1], z_recv.at[d - 1], behind[d])
        for d in (1, 2, 3)
    ]
    for k in range(4):
        cols = slice(k * wide, (k + 1) * wide)
        share = jnp.dot(gate_delta, gate_w[:, cols], preferred_element_type=F32)
        share += jnp.dot(up_delta, up_w[:, cols], preferred_element_type=F32)
        share = share.reshape(8, 16, wide)
        core_out[k] = share[4:8].astype(BF)
        to_core[k].start()
        sums[k] = share[0:4]

    def weight_grad(out, delta, by_tokens):
        for c in range(4):
            cols = slice(c * wide, (c + 1) * wide)
            out[:, cols] = contract_first(delta, by_tokens(c)).astype(BF)

    for k in range(4):
        leave, stay = ((2, 3), (0, 1)) if k % 2 == 0 else ((1, 3), (0, 2))
        to_core[k].wait_recv()
        for j in range(2):
            first_out[k, j] = (sums[k, leave[j]] + core_in[k, leave[j]].astype(F32)).astype(BF)
        first[k].start()
        for j in range(2):
            halves[k, j] = sums[k, stay[j]] + core_in[k, stay[j]].astype(F32)
    weight_grad(gate_grad_ref, gate_delta, inputs_of)
    for k in range(4):
        first[k].wait_recv()
        second_out[k] = (halves[k, 1] + first_in[k, 1].astype(F32)).astype(BF)
        second[k].start()
        blocks[k] = halves[k, 0] + first_in[k, 0].astype(F32)
    weight_grad(up_grad_ref, up_delta, inputs_of)
    for k in range(4):
        second[k].wait_recv()
    stripes = [blocks[k] + second_in[k].astype(F32) for k in range(4)]
    for d in (3, 2, 1, 0):
        folded = jnp.concatenate([stripe[4 * d:4 * d + 4, :] for stripe in stripes], axis=0)
        if d == 0:
            last_keep[...] = folded
        else:
            last_out[d - 1] = folded.astype(BF)
            last[d - 1].start()
    weight_grad(down_grad_ref, hidden, lambda c: weighted_all[:, c * wide:(c + 1) * wide])
    final = last_keep[...]
    for d in range(3):
        last[d].wait_recv()
        final += last_in[d].astype(F32)
    for k in range(4):
        input_grad_ref[:, k * wide:(k + 1) * wide] = final[4 * k:4 * k + 4, :].astype(BF)

    for copy in along_z + to_x + to_y + to_d:
        copy.wait_send()
    for slot in range(4):
        to_mate(slot, 0).wait_send()
        to_mate(slot, 1).wait_send()
    for copy in to_core + first + second + last:
        copy.wait_send()


def fused(
    hidden_in, out_grad, step_ids, segment_ids, advantage_codes, gate_weight, up_weight, down_weight
):
    features, units = gate_weight.shape
    local_tokens = hidden_in.shape[0]
    tokens = 32 * local_tokens
    wide = features // 4
    vmem = pl.BlockSpec(memory_space=pltpu.VMEM)
    hbm = pl.BlockSpec(memory_space=pl.ANY)
    dma = pltpu.SemaphoreType.DMA
    shapes = (
        jax.ShapeDtypeStruct(hidden_in.shape, BF),
        jax.ShapeDtypeStruct((units, features), BF),
        jax.ShapeDtypeStruct((units, features), BF),
        jax.ShapeDtypeStruct((units, features), BF),
    )
    input_grad, gate_grad, up_grad, down_grad = pl.pallas_call(
        gather_kernel,
        out_shape=shapes,
        in_specs=[hbm] * 8,
        out_specs=(vmem,) * 4,
        scratch_shapes=[
            pltpu.VMEM((units, features), BF),
            pltpu.VMEM((units, features), BF),
            pltpu.VMEM((units, features), BF),
            pltpu.VMEM((tokens, features), BF),
            pltpu.VMEM((local_tokens, features), BF),
            pltpu.VMEM((local_tokens, features), BF),
            pltpu.SMEM((local_tokens,), jnp.int32),
            pltpu.SMEM((local_tokens,), jnp.int32),
            pltpu.SMEM((local_tokens,), jnp.int32),
            pltpu.VMEM((8, 4, 16, LANES + 2 * wide), BF),
            pltpu.VMEM((8, 16, LANES + 2 * features), BF),
            pltpu.VMEM((4, 4, 16, wide), BF),
            pltpu.VMEM((4, 4, 16, wide), BF),
            pltpu.VMEM((4, 4, 16, wide), F32),
            pltpu.VMEM((4, 2, 16, wide), BF),
            pltpu.VMEM((4, 2, 16, wide), BF),
            pltpu.VMEM((4, 2, 16, wide), F32),
            pltpu.VMEM((4, 16, wide), BF),
            pltpu.VMEM((4, 16, wide), BF),
            pltpu.VMEM((4, 16, wide), F32),
            pltpu.VMEM((16, wide), F32),
            pltpu.VMEM((3, 16, wide), BF),
            pltpu.VMEM((3, 16, wide), BF),
            dma((8,)),
            dma((3,)), dma((3,)),
            dma((4,)), dma((4,)), dma((4,)), dma((4,)), dma((4,)), dma((4,)),
            dma((8,)), dma((8,)),
            dma((4,)), dma((4,)), dma((4,)), dma((4,)), dma((4,)), dma((4,)),
            dma((3,)), dma((3,)),
        ],
        compiler_params=pltpu.CompilerParams(
            collective_id=0, has_side_effects=True, vmem_limit_bytes=36 * 1024 * 1024
        ),
        name="gather_and_sum",
    )(*[
        pltpu.with_memory_space_constraint(value, pltpu.HBM)
        for value in (
            hidden_in, out_grad, step_ids, segment_ids, advantage_codes,
            gate_weight.T, up_weight.T, down_weight,
        )
    ])
    return (input_grad, gate_grad.T, up_grad.T, down_grad)


def local(
    hidden_in, out_grad, step_ids, segment_ids, advantage_codes, gate_weight, up_weight, down_weight
):
    inputs_all, grads_all = (
        lax.all_gather(hidden_in, "ffn", axis=0, tiled=True),
        lax.all_gather(out_grad, "ffn", axis=0, tiled=True),
    )
    labels = lax.all_gather(
        jnp.stack([step_ids, segment_ids, advantage_codes]), "ffn", axis=1, tiled=True
    )
    advantage = advantage_weights(labels[0], labels[1], labels[2])
    weighted = (advantage[:, None] * grads_all.astype(jnp.float32)).astype(jnp.bfloat16)
    gate_part = jnp.dot(inputs_all, gate_weight, preferred_element_type=jnp.float32)
    up_part = jnp.dot(inputs_all, up_weight, preferred_element_type=jnp.float32)
    gate_pre, up_pre = lax.psum((gate_part, up_part), "mp")
    sigma = jax.nn.sigmoid(gate_pre)
    hidden = (gate_pre * sigma * up_pre).astype(jnp.bfloat16)
    hidden_grad = lax.psum(contract_last(weighted, down_weight), "mp")
    up_delta = (hidden_grad * gate_pre * sigma).astype(jnp.bfloat16)
    gate_delta = (hidden_grad * up_pre * sigma * (1.0 + gate_pre * (1.0 - sigma))).astype(
        jnp.bfloat16
    )
    down_grad = contract_first(hidden, weighted).astype(jnp.bfloat16)
    gate_grad = contract_first(inputs_all, gate_delta).astype(jnp.bfloat16)
    up_grad = contract_first(inputs_all, up_delta).astype(jnp.bfloat16)
    partial_grad = contract_last(gate_delta, gate_weight) + contract_last(up_delta, up_weight)
    input_grad = lax.psum_scatter(partial_grad, "ffn", scatter_dimension=0, tiled=True)
    return (input_grad.astype(jnp.bfloat16), gate_grad, up_grad, down_grad)


def solution(mesh):
    in_specs = (
        P(("groups", "ffn"), "mp"),
        P(("groups", "ffn"), "mp"),
        P(("groups", "ffn")),
        P(("groups", "ffn")),
        P(("groups", "ffn")),
        P("mp", "ffn"),
        P("mp", "ffn"),
        P("ffn", "mp"),
    )
    out_specs = (
        P(("groups", "ffn"), "mp"),
        P(("groups", "mp"), "ffn"),
        P(("groups", "mp"), "ffn"),
        P(("groups", "ffn"), "mp"),
    )
    whole = mesh.shape["groups"] == 1 and mesh.shape["mp"] == 1 and mesh.shape["ffn"] == 32
    return jax.shard_map(fused if whole else local, mesh=mesh, in_specs=in_specs, out_specs=out_specs, check_vma=False)
```
